512 devices in a mesh: dp: 32 (over z, x_hi), tensor: 16 (over x_lo, y, core).
Axes of the slice: x: 4 (x_hi: 2, x_lo: 2; x = x_hi * 2 + x_lo), y: 4, z: 16, core: 2. Of those that a mesh axis runs over, the one named last changes fastest.
Arguments:
- acts: bfloat16 [32768, 28672], P('dp', 'tensor'), may hold values from -6 to 6
Outputs:
- factor_tiles: float32 [896, 16, 2, 896], P('dp', 'tensor')
The draws below stay inside these ranges and needn't reach their ends.
All inputs are finite; a program needn't handle non-finite values.
Results may differ from the reference program's by a relative error of at most 0.0003.
Values may be sent and summed in bfloat16 or wider, within the bound.
A program may use at most 64 MiB of HBM per device.

```python
import jax
import jax.numpy as jnp
from jax import lax

FF = 28672
FROWS = 896
COLS = 896
STEPS = 2
SLAB = 1792
TOKENS = 32768
N_TENSOR = 16


def spiked(entries, rng, source, target, blocks, factor):
    owner, partner = [(jnp.arange(entries.shape[dim]) // (entries.shape[dim] // blocks)).reshape([-1 if axis == dim else 1 for axis in range(entries.ndim)]) for dim in (source, target)]
    chosen = jax.random.permutation(rng, blocks)[partner]
    strong = (owner == chosen) | (owner == (partner + blocks // 2) % blocks)
    return jnp.where(strong, factor * entries, entries)


def block_levels(own_key, extent, cuts, low, top_value):
    loudness = 1.0
    for position, shards_of in cuts:
        draws = jax.random.uniform(jax.random.fold_in(jax.random.fold_in(own_key, 6), position), (shards_of,), jnp.float32, low / len(cuts), top_value / len(cuts))
        loudness = loudness * jnp.repeat(jnp.exp(draws), extent[position] // shards_of).reshape((-1,) + (1,) * (len(extent) - 1 - position))
    return loudness


def bell_draw_with(own_key, dims, scale, bound, shards, heavy, kind=jnp.bfloat16):
    values = scale * jax.random.normal(own_key, dims, jnp.float32)
    if shards:
        values = values * block_levels(own_key, dims, shards, -0.22, 0.18)
    return jnp.clip(spiked(values, jax.random.fold_in(own_key, 3), *heavy), -bound, bound).astype(kind)


def setup_inputs(seed: int = 0) -> dict:
    key_list = jax.random.split(jax.random.key(seed), 2)
    return {
        "acts": bell_draw_with(key_list[0], (TOKENS, FF), 1.0, 6.0, ((0, 32), (1, 16)), (0, 1, 32, 2.75)),
    }


def reference(acts):
    scale = 1.0 / TOKENS
    rows_all = []
    for t in range(N_TENSOR):
        window = acts[:, t * SLAB:t * SLAB + FROWS]
        tiles = []
        for s in range(STEPS):
            u = (t - s) % N_TENSOR
            other = acts[:, u * SLAB:u * SLAB + COLS]
            product = lax.dot_general(window, other, (((0,), (0,)), ((), ())), preferred_element_type=jnp.float32)
            tiles.append(product * scale)
        rows_all.append(jnp.stack(tiles, axis=1))
    return jnp.stack(rows_all, axis=1)
```

```python
import jax
import jax.numpy as jnp
from jax import lax
from jax.experimental import pallas as pl
from jax.experimental.pallas import tpu as pltpu
from jax.sharding import PartitionSpec as P

ROWS = 896
COLS = 896
LANES = 128
MESH = pl.DeviceIdType.MESH
TN = (((0,), (0,)), ((), ()))

POWER = 17
TOP = 2.0**7.375

STREAMS = ((0, 0, 4), (0, 4, 3), (1, 0, 4), (1, 4, 3))
LAGS = ((0, 0, 1, 2), (0, 0, 2, 4))
SCALE_ROWS = 16


def round_up(n, m):
    return (n + m - 1) // m * m


def encode(value, factor):
    u = value * factor
    u2 = u * u
    u4 = u2 * u2
    u8 = u4 * u4
    return u8 * u8 * u


def decode(code, factor):
    y = code.astype(jnp.float32)
    size = jnp.exp2(jnp.log2(jnp.abs(y)) * (1.0 / POWER)) * factor
    return jnp.where(y == 0.0, 0.0, jnp.where(y < 0.0, -size, size))


def groups(blocks):
    out = [(2 * i, 2) for i in range(blocks // 2)]
    if blocks % 2:
        out.append((blocks - 1, 1))
    return out


def lane_max(values):
    n = values.shape[0] // 8
    return jnp.max(jnp.abs(values).reshape(n, 8, LANES), axis=0)


def scale_of(top):
    top = jnp.max(top, axis=0, keepdims=True)
    return (top * 1.008 + 1e-36).astype(jnp.bfloat16).astype(jnp.float32)


def kernel(nz, acts_ref, out_ref, mine, other, part0, part1, held, *rest):
    ns = len(STREAMS)
    got = rest[:ns]
    put = rest[ns : 2 * ns]
    xgot = rest[2 * ns : 3 * ns]
    xput = rest[3 * ns : 4 * ns]
    kept = rest[4 * ns : 5 * ns]
    load_sem, wsend, wrecv, rsend, rrecv, xsend, xrecv = rest[5 * ns :]
    parts = (part0, part1)
    chunk = ROWS // nz
    half = chunk // 2
    wide = round_up(half, 8)

    dp = lax.axis_index("dp")
    t = lax.axis_index("tensor")
    ndp = 2 * nz
    nt = lax.axis_size("tensor")
    z, xh = dp // 2, lax.rem(dp, 2)
    core = lax.rem(t, 2)
    ahead = (lax.rem(dp + 2, ndp), t)
    behind = (lax.rem(dp + ndp - 2, ndp), t)
    across = (dp + 1 - 2 * xh, t)
    right = (dp, lax.rem(t + 1, nt))
    left = (dp, lax.rem(t + nt - 1, nt))

    load = pltpu.make_async_copy(acts_ref.at[:, 0:COLS], mine, load_sem)
    load.start()
    barrier = pltpu.get_barrier_semaphore()
    for device in (ahead, behind, across, right, left):
        pl.semaphore_signal(barrier, inc=1, device_id=device, device_id_type=MESH)
    load.wait()
    pl.semaphore_wait(barrier, 5)

    windows = []
    for i, (a, b) in enumerate(((0, 512), (512, 896))):
        windows.append(
            pltpu.make_async_remote_copy(
                src_ref=mine.at[:, a:b],
                dst_ref=other.at[:, a:b],
                send_sem=wsend.at[i],
                recv_sem=wrecv.at[i],
                device_id=right,
                device_id_type=MESH,
            )
        )
    for copy in windows:
        copy.start()

    part0[...] = lax.dot_general(mine[...], mine[...], TN, preferred_element_type=jnp.float32)

    def hops(i, d):
        return nz // 2 - (d + i) % 2

    def message(i, d, k):
        return pltpu.make_async_remote_copy(
            src_ref=put[i].at[d, k],
            dst_ref=got[i].at[d, k],
            send_sem=rsend.at[i, d, k],
            recv_sem=rrecv.at[i, d, k],
            device_id=behind if d else ahead,
            device_id_type=MESH,
        )

    def swap(i):
        return pltpu.make_async_remote_copy(
            src_ref=xput[i],
            dst_ref=xgot[i],
            send_sem=xsend.at[i],
            recv_sem=xrecv.at[i],
            device_id=across,
            device_id_type=MESH,
        )

    def partial(i, g, n, owner):
        tile, first, _ = STREAMS[i]
        rows = pl.ds(pl.multiple_of(owner * chunk, 8), chunk)
        pieces = [
            parts[tile][rows, (first + g + j) * LANES : (first + g + j + 1) * LANES]
            for j in range(n)
        ]
        return jnp.concatenate(pieces, axis=0) if n > 1 else pieces[0]

    def factor_in(ref, at):
        return ref[at : at + SCALE_ROWS, :].astype(jnp.float32)[0:1] * (1.0 / TOP)

    def unpack(ref, a, n, factor):
        size = round_up(n, 16)
        return decode(ref[a : a + size, :], factor)[:n]

    def pack(src, ref, spans, top, tail):
        scale = scale_of(top)
        factor = TOP / scale
        for a, n in spans:
            ref[a : a + n, :] = encode(src[a : a + n, :], factor).astype(jnp.bfloat16)
        ref[tail : tail + SCALE_ROWS, :] = jnp.broadcast_to(scale, (SCALE_ROWS, LANES)).astype(
            jnp.bfloat16
        )

    def step(i, d, k):
        blocks = STREAMS[i][2]
        length = hops(i, d)
        sign = -1 if d else 1
        owner = lax.rem(z + sign * (length - k) + 2 * nz, nz)
        body = round_up(blocks * chunk, 16)

        @pl.when(k == 0)
        def _():
            for g, n in groups(blocks):
                held[g * chunk : (g + n) * chunk, :] = partial(i, g, n, owner)

        @pl.when(k > 0)
        def _():
            message(i, d, k - 1).wait_recv()
            ref = got[i].at[d, k - 1]
            factor = factor_in(ref, body)
            for g, n in groups(blocks):
                held[g * chunk : (g + n) * chunk, :] = partial(i, g, n, owner) + unpack(
                    ref, g * chunk, n * chunk, factor
                )

        top = jnp.zeros((8, LANES), jnp.float32)
        for g, n in groups(blocks):
            top = jnp.maximum(top, lane_max(held[g * chunk : (g + n) * chunk, :]))
        spans = [(g * chunk, round_up(n * chunk, 16)) for g, n in groups(blocks)]
        pack(held, put[i].at[d, k], spans, top, body)
        message(i, d, k).start()

    def finish(i):
        blocks = STREAMS[i][2]
        body = round_up(blocks * chunk, 16)
        refs = []
        for d in range(2):
            last = hops(i, d) - 1
            message(i, d, last).wait_recv()
            refs.append(got[i].at[d, last])
        factors = [factor_in(ref, body) for ref in refs]
        top = jnp.zeros((8, LANES), jnp.float32)
        for g, n in groups(blocks):
            total = partial(i, g, n, z)
            for ref, factor in zip(refs, factors):
                total = total + unpack(ref, g * chunk, n * chunk, factor)
            for j in range(n):
                low = total[j * chunk : j * chunk + wide]
                high = total[(j + 1) * chunk - wide : (j + 1) * chunk]
                at = (g + j) * wide
                kept[i][at : at + wide, :] = jnp.where(xh == 0, low, high)
                away = jnp.where(xh == 0, high, low)
                held[at : at + wide, :] = away
                top = jnp.maximum(top, lane_max(away))
        spans = [(j * wide, wide) for j in range(blocks)]
        pack(held, xput[i], spans, top, blocks * wide)
        swap(i).start()

    def deliver(i):
        tile, first, blocks = STREAMS[i]
        swap(i).wait_recv()
        factor = factor_in(xgot[i], blocks * wide)
        inverse = 1.0 / (1024 * ndp)
        for j in range(blocks):
            at = j * wide
            total = (kept[i][at : at + wide, :] + unpack(xgot[i], at, wide, factor)) * inverse
            value = jnp.where(xh == 0, total[:half], total[wide - half :])
            out_ref[pl.ds(2 * (first + j) + tile, half, stride=2 * (COLS // LANES)), :] = value

    def lag(i):
        return jnp.where(core == 0, LAGS[1][i], LAGS[0][i])

    last = nz // 2

    def tick(now, _):
        for i, (tile, first, blocks) in enumerate(STREAMS):
            k = now - lag(i)
            if tile:
                a, b = first * LANES, (first + blocks) * LANES

                @pl.when(k == 0)
                def _():
                    windows[i - 2].wait_recv()
                    part1[:, a:b] = lax.dot_general(
                        mine[...], other[:, a:b], TN, preferred_element_type=jnp.float32
                    )

            for d in range(2):

                @pl.when((k >= 0) & (k < hops(i, d)))
                def _():
                    step(i, d, k)

            @pl.when(k == last)
            def _():
                finish(i)

            @pl.when(k == last + 1)
            def _():
                deliver(i)

        return 0

    lax.fori_loop(0, max(map(max, LAGS)) + last + 2, tick, 0)

    for copy in windows:
        copy.wait_send()
    for i in range(ns):
        for d in range(2):
            for k in range(hops(i, d)):
                message(i, d, k).wait_send()
        swap(i).wait_send()


def per_device(acts):
    nz = lax.axis_size("dp") // 2
    chunk = ROWS // nz
    half = chunk // 2
    wide = round_up(half, 8)
    depth = nz // 2
    ns = len(STREAMS)
    body = [round_up(b * chunk, 16) + SCALE_ROWS for _, _, b in STREAMS]
    xbody = [b * wide + SCALE_ROWS for _, _, b in STREAMS]
    scratch = [
        pltpu.VMEM((acts.shape[0], COLS), jnp.bfloat16),
        pltpu.VMEM((acts.shape[0], COLS), jnp.bfloat16),
        pltpu.VMEM((ROWS, COLS), jnp.float32),
        pltpu.VMEM((ROWS, COLS), jnp.float32),
        pltpu.VMEM((max(body), LANES), jnp.float32),
    ]
    scratch += [pltpu.VMEM((2, depth, n, LANES), jnp.bfloat16) for n in body] * 2
    scratch += [pltpu.VMEM((n, LANES), jnp.bfloat16) for n in xbody] * 2
    scratch += [pltpu.VMEM((n - SCALE_ROWS, LANES), jnp.float32) for n in xbody]
    dma = pltpu.SemaphoreType.DMA
    scratch += [dma, dma((2,)), dma((2,)), dma((ns, 2, depth)), dma((ns, 2, depth)), dma((ns,)), dma((ns,))]
    flat = pl.pallas_call(
        lambda *refs: kernel(nz, *refs),
        out_shape=jax.ShapeDtypeStruct((half * 2 * (COLS // LANES), LANES), jnp.float32),
        in_specs=[pl.BlockSpec(memory_space=pl.ANY)],
        out_specs=pl.BlockSpec(memory_space=pltpu.VMEM),
        scratch_shapes=scratch,
        compiler_params=pltpu.CompilerParams(
            collective_id=0, has_side_effects=True, vmem_limit_bytes=48 * 2**20
        ),
        cost_estimate=pl.CostEstimate(
            flops=4 * ROWS * COLS * acts.shape[0], bytes_accessed=2 * acts.size, transcendentals=0
        ),
    )(acts)
    tiles = flat.reshape(half, COLS // LANES, 2, LANES).transpose(0, 2, 1, 3)
    return tiles.reshape(half, 1, 2, COLS)


def solution(mesh):
    return jax.shard_map(
        per_device,
        mesh=mesh,
        in_specs=(P("dp", "tensor"),),
        out_specs=P("dp", "tensor", None, None),
        check_vma=False,
    )
```

```python
import jax
import jax.numpy as jnp
from jax import lax
from jax.experimental import pallas as pl
from jax.experimental.pallas import tpu as pltpu
from jax.sharding import PartitionSpec as P

ROWS = 896
COLS = 896
LANES = 128
BLOCKS = COLS // LANES
MESH = pl.DeviceIdType.MESH
TN = (((0,), (0,)), ((), ()))

POWER = 17
TOP = 2.0**7.375

STREAMS = ((0, 0, 4), (0, 4, 3), (1, 0, 4), (1, 4, 3))
STARTS = ((0, 0, 0, 0), (0, 0, 2, 5))
CHAINS = ((8, 8, 8, 8), (8, 8, 8, 4))
PIECES = 2
JUMPS = (1, 5)
TICKS = 12


def by_core(core, table):
    return jnp.where(core == 0, table[0], table[1])


def scaled(value, factor):
    return (value.reshape(value.shape[0] // 8, 8, LANES) * factor).reshape(value.shape)


def encode(value, factor):
    u = scaled(value, factor)
    u2 = u * u
    u4 = u2 * u2
    u8 = u4 * u4
    return u8 * u8 * u


def decode(code, factor):
    y = code.astype(jnp.float32)
    size = scaled(jnp.exp2(jnp.log2(jnp.abs(y)) * (1.0 / POWER)), factor)
    return jnp.where(y < 0.0, -size, size)


def tops(values):
    out = None
    for value in values:
        top = jnp.max(jnp.abs(value).reshape(value.shape[0] // 8, 8, LANES), axis=0)
        out = top if out is None else jnp.maximum(out, top)
    return out


class Packet:
    def __init__(self, sizes):
        self.spans = []
        at = 0
        for n in sizes:
            self.spans.append((at, n))
            at += n
        self.body = at
        self.rows = (at // 16 + 1) * 16
        self.tail = self.rows - at

    def read(self, ref):
        bound = ref[self.rows - 16 : self.rows, :].astype(jnp.float32)[8:]
        factor = bound * (1.0 / TOP)
        values = [decode(ref[at : at + (n + 15) // 16 * 16, :], factor)[:n] for at, n in self.spans]
        return values, bound

    def write(self, values, ref, bound):
        bound = (bound * 1.008 + 1e-36).astype(jnp.bfloat16).astype(jnp.float32)
        factor = TOP / bound
        rest = jnp.concatenate([bound] * (self.tail // 8), axis=0)
        for value, (at, n) in zip(values, self.spans):
            code = encode(value, factor)
            if n % 16:
                code = jnp.concatenate([code, rest], axis=0)
            ref[at : at + code.shape[0], :] = code.astype(jnp.bfloat16)
        if self.body % 16 == 0:
            ref[self.body : self.rows, :] = rest.astype(jnp.bfloat16)


def add(some, more):
    return [x + y for x, y in zip(some, more)]


PACKETS = tuple(Packet((112,) * (n // 2) + (56,) * (n % 2)) for _, _, n in STREAMS)
SWAPS = tuple(Packet((32,) * n) for _, _, n in STREAMS)


def kernel(nz, acts_ref, out_ref, mine, pair, other, part0, part1, peaks, *rest):
    ns = len(STREAMS)
    got, put, late_got, late_put = (rest[k * ns : (k + 1) * ns] for k in range(4))
    kept, load_sem, psend, precv, wsend, wrecv, rsend, rrecv, lsend, lrecv = rest[4 * ns :]
    parts = (part0, part1)
    chunk = ROWS // nz
    depth = nz // 2

    dp = lax.axis_index("dp")
    t = lax.axis_index("tensor")
    ndp = 2 * nz
    nt = lax.axis_size("tensor")
    z, xh = lax.div(dp, 2), lax.rem(dp, 2)
    core = lax.rem(t, 2)
    even = xh == 0

    def along(hops):
        return (lax.rem(dp + 2 * hops + 2 * ndp, ndp), t)

    twin = dp + 1 - 2 * xh
    across = (twin, t)
    mate = t + 1 - 2 * core
    right, left = lax.rem(t + 2, nt), lax.rem(t + nt - 2, nt)

    load = pltpu.make_async_copy(acts_ref.at[:, 0:COLS], mine, load_sem)
    load.start()
    barrier = pltpu.get_barrier_semaphore()
    partners = [along(sign * jump) for jump in JUMPS for sign in (1, -1)]
    partners += [across, (dp, mate), (twin, mate), (dp, right), (dp, left)]
    for device in partners:
        pl.semaphore_signal(barrier, inc=1, device_id=device, device_id_type=MESH)
    load.wait()
    for i in range(ns):
        for d in range(2):
            got[i][d, depth] = jnp.zeros(got[i].shape[2:], jnp.bfloat16)

    def own_rows(i, owner):
        tile, first, _ = STREAMS[i]
        rows = pl.ds(pl.multiple_of(owner * chunk, 8), chunk)
        values = []
        for at, n in PACKETS[i].spans:
            j = first + at // chunk
            pieces = [
                parts[tile][rows, (j + m) * LANES : (j + m + 1) * LANES] for m in range(n // chunk)
            ]
            values.append(jnp.concatenate(pieces, axis=0) if len(pieces) > 1 else pieces[0])
        return values

    second = [tile for tile, _, _ in STREAMS].index(1)

    def columns(i):
        _, first, blocks = STREAMS[i]
        return first * LANES, (first + blocks) * LANES

    def multiply(i, left_ref, right_ref):
        a, b = columns(i)
        parts[STREAMS[i][0]][:, a:b] = lax.dot_general(
            left_ref[...], right_ref[:, a:b], TN, preferred_element_type=jnp.float32
        )

    def measure(i):
        def peak(owner, _):
            peaks[i, owner] = tops(own_rows(i, owner))
            return 0

        lax.fori_loop(0, nz, peak, 0)

    for i in range(second):
        multiply(i, mine, mine)
        measure(i)
    pl.semaphore_wait(barrier, len(partners))

    exchange = pltpu.make_async_remote_copy(
        src_ref=mine,
        dst_ref=pair,
        send_sem=psend,
        recv_sem=precv,
        device_id=(dp, mate),
        device_id_type=MESH,
    )
    exchange.start()

    def window(i):
        a, b = columns(i)
        return pltpu.make_async_remote_copy(
            src_ref=mine.at[:, a:b],
            dst_ref=other.at[:, a:b],
            send_sem=wsend.at[i],
            recv_sem=wrecv.at[i],
            device_id=(dp, right),
            device_id_type=MESH,
        )

    @pl.when(core == 1)
    def _():
        for i in range(second, ns):
            window(i).start()

    def reach(i, d):
        return depth - lax.rem(d + i, 2)

    def chain(i):
        return by_core(core, [c[i] for c in CHAINS])

    def message(i, d, hop, target):
        return pltpu.make_async_remote_copy(
            src_ref=put[i].at[d, hop - 1],
            dst_ref=got[i].at[d, hop - 1],
            send_sem=rsend.at[i, d, hop - 1],
            recv_sem=rrecv.at[i, d, hop - 1],
            device_id=target,
            device_id_type=MESH,
        )

    def late(i, which):
        target = (twin if which else dp, mate if STREAMS[i][0] else t)
        return pltpu.make_async_remote_copy(
            src_ref=late_put[i].at[which],
            dst_ref=late_got[i].at[which],
            send_sem=lsend.at[i, which],
            recv_sem=lrecv.at[i, which],
            device_id=target,
            device_id_type=MESH,
        )

    def step(i, d, hop, length):
        sign = 1 - 2 * d
        owner = lax.rem(z + sign * hop + nz, nz)
        outermost = (hop == reach(i, d)) | (lax.rem(hop, length) == 0)

        @pl.when(jnp.logical_not(outermost))
        def _():
            message(i, d, hop + 1, across).wait_recv()

        values, bound = own_rows(i, owner), peaks[i, owner]
        more, more_bound = PACKETS[i].read(got[i].at[d, jnp.where(outermost, depth, hop)])
        PACKETS[i].write(add(values, more), put[i].at[d, hop - 1], bound + more_bound)
        jump = jnp.where(lax.rem(hop, length) == 1, hop, 1)
        message(i, d, hop, along(sign * jump)).start()

    def tick_of(i, k):
        length = chain(i)

        def one(j, _):
            d, m = lax.rem(j, 2), lax.div(j, 2)
            hop = (m + 1) * length - k

            @pl.when((k >= 0) & (k < length) & (hop <= reach(i, d)))
            def _():
                step(i, d, hop, length)

            return 0

        lax.fori_loop(0, 2 * PIECES, one, 0)

    def gather(i):
        length = chain(i)
        values, bound = own_rows(i, z), peaks[i, z]
        for m in range(PIECES):
            for d in range(2):
                hop = m * length + 1
                here = hop <= reach(i, d)

                @pl.when(here)
                def _():
                    message(i, d, hop, across).wait_recv()

                more, more_bound = PACKETS[i].read(got[i].at[d, jnp.where(here, hop - 1, depth)])
                values, bound = add(values, more), bound + more_bound
        return values, bound

    inverse = 1.0 / (1024 * ndp)
    stride = 2 * BLOCKS

    def finish(i):
        tile, _, blocks = STREAMS[i]
        values, bound = gather(i)
        total = jnp.concatenate(values, axis=0)
        here, away = [], []
        for block in range(blocks):
            low = total[block * chunk : block * chunk + 32]
            high = total[(block + 1) * chunk - 32 : (block + 1) * chunk]
            here.append(jnp.where(even, low, high))
            away.append(jnp.where(even, high, low))
        SWAPS[i].write(away, late_put[i].at[1], bound)
        late(i, 1).start()
        if tile:
            SWAPS[i].write(here, late_put[i].at[0], bound)
            late(i, 0).start()
        else:
            for block in range(blocks):
                at = 32 * (STREAMS[i][1] + block)
                kept[at : at + 32, :] = here[block]

    def deliver(i):
        tile, first, blocks = STREAMS[i]
        late(i, 1).wait_recv()
        values, _ = SWAPS[i].read(late_got[i].at[1])
        if tile:
            late(i, 0).wait_recv()
            others, _ = SWAPS[i].read(late_got[i].at[0])
        else:
            others = [kept[32 * j : 32 * j + 32, :] for j in range(first, first + blocks)]
        for block in range(blocks):
            total = values[block] + others[block]
            value = jnp.where(even, total[:28], total[4:])
            out_ref[pl.ds(2 * (first + block) + tile, 28, stride=stride), :] = value * inverse

    def tick(now, _):
        for i in range(ns):
            k = now - by_core(core, [s[i] for s in STARTS])
            length = chain(i)

            if STREAMS[i][0]:

                @pl.when(k == 0)
                def _():
                    if i == second:
                        exchange.wait_recv()

                    @pl.when(core == 0)
                    def _():
                        multiply(i, pair, mine)

                    @pl.when(core == 1)
                    def _():
                        window(i).wait_recv()
                        multiply(i, pair, other)

                    measure(i)

            tick_of(i, k)

            @pl.when(k == length)
            def _():
                finish(i)

            if STREAMS[i][0] == 0:

                @pl.when(k == length + 1)
                def _():
                    deliver(i)

        return 0

    lax.fori_loop(0, TICKS, tick, 0)

    for i in range(second, ns):
        deliver(i)
    exchange.wait_send()

    @pl.when(core == 1)
    def _():
        for i in range(second, ns):
            window(i).wait_send()

    for i in range(ns):
        for d in range(2):

            def sent(k, _):
                message(i, d, k + 1, across).wait_send()
                return 0

            lax.fori_loop(0, depth - (d + i) % 2, sent, 0)
        late(i, 1).wait_send()
        if STREAMS[i][0]:
            late(i, 0).wait_send()


def per_device(acts):
    nz = lax.axis_size("dp") // 2
    depth = nz // 2
    ns = len(STREAMS)
    ring = [p.rows for p in PACKETS]
    swaps = [p.rows for p in SWAPS]
    scratch = [
        pltpu.VMEM((acts.shape[0], COLS), jnp.bfloat16),
        pltpu.VMEM((acts.shape[0], COLS), jnp.bfloat16),
        pltpu.VMEM((acts.shape[0], COLS), jnp.bfloat16),
        pltpu.VMEM((ROWS, COLS), jnp.float32),
        pltpu.VMEM((ROWS, COLS), jnp.float32),
        pltpu.VMEM((ns, nz, 8, LANES), jnp.float32),
    ]
    scratch += [pltpu.VMEM((2, depth + 1, n, LANES), jnp.bfloat16) for n in ring]
    scratch += [pltpu.VMEM((2, depth, n, LANES), jnp.bfloat16) for n in ring]
    scratch += [pltpu.VMEM((2, n, LANES), jnp.bfloat16) for n in swaps] * 2
    scratch += [pltpu.VMEM((32 * BLOCKS, LANES), jnp.float32)]
    dma = pltpu.SemaphoreType.DMA
    scratch += [dma, dma, dma, dma((ns,)), dma((ns,)), dma((ns, 2, depth)), dma((ns, 2, depth)), dma((ns, 2)), dma((ns, 2))]
    half = ROWS // (2 * nz)
    flat = pl.pallas_call(
        lambda *refs: kernel(nz, *refs),
        out_shape=jax.ShapeDtypeStruct((half * 2 * BLOCKS, LANES), jnp.float32),
        in_specs=[pl.BlockSpec(memory_space=pl.ANY)],
        out_specs=pl.BlockSpec(memory_space=pltpu.VMEM),
        scratch_shapes=scratch,
        compiler_params=pltpu.CompilerParams(
            collective_id=0, has_side_effects=True, vmem_limit_bytes=52 * 2**20
        ),
        cost_estimate=pl.CostEstimate(
            flops=4 * ROWS * COLS * acts.shape[0], bytes_accessed=2 * acts.size, transcendentals=0
        ),
    )(acts)
    tiles = flat.reshape(half, BLOCKS, 2, LANES).transpose(0, 2, 1, 3)
    return tiles.reshape(half, 1, 2, COLS)


def solution(mesh):
    return jax.shard_map(
        per_device,
        mesh=mesh,
        in_specs=(P("dp", "tensor"),),
        out_specs=P("dp", "tensor", None, None),
        check_vma=False,
    )
```

```python
import jax
import jax.numpy as jnp
from jax import lax
from jax.experimental import pallas as pl
from jax.experimental.pallas import tpu as pltpu
from jax.sharding import PartitionSpec as P

ROWS = 896
COLS = 896
LANES = 128
BLOCKS = COLS // LANES
MESH = pl.DeviceIdType.MESH
TN = (((0,), (0,)), ((), ()))

POWER = 17
TOP = 2.0**7.375

STREAMS = ((0, 0, 4), (0, 4, 3), (1, 0, 3), (1, 3, 4))
STARTS = ((0, 0, 0, 0), (0, 0, 2, 5))
CHAINS = ((8, 8, 8, 8), (8, 8, 8, 4))
PIECES = 2
JUMPS = (1, 5)
TICKS = 12


def by_core(core, table):
    return jnp.where(core == 0, table[0], table[1])


def scaled(value, factor):
    return (value.reshape(value.shape[0] // 8, 8, LANES) * factor).reshape(value.shape)


def encode(value, factor):
    u = scaled(value, factor)
    u2 = u * u
    u4 = u2 * u2
    u8 = u4 * u4
    return u8 * u8 * u


def decode(code, factor):
    y = code.astype(jnp.float32)
    size = scaled(jnp.exp2(jnp.log2(jnp.abs(y)) * (1.0 / POWER)), factor)
    return jnp.where(y < 0.0, -size, size)


def tops(values):
    out = None
    for value in values:
        top = jnp.max(jnp.abs(value).reshape(value.shape[0] // 8, 8, LANES), axis=0)
        out = top if out is None else jnp.maximum(out, top)
    return out


class Packet:
    def __init__(self, sizes):
        self.spans = []
        at = 0
        for n in sizes:
            self.spans.append((at, n))
            at += n
        self.body = at
        self.rows = (at // 16 + 1) * 16
        self.tail = self.rows - at

    def read(self, ref):
        bound = ref[self.rows - 16 : self.rows, :].astype(jnp.float32)[8:]
        factor = bound * (1.0 / TOP)
        values = [decode(ref[at : at + (n + 15) // 16 * 16, :], factor)[:n] for at, n in self.spans]
        return values, bound

    def write(self, values, ref, bound):
        bound = (bound * 1.008 + 1e-36).astype(jnp.bfloat16).astype(jnp.float32)
        factor = TOP / bound
        rest = jnp.concatenate([bound] * (self.tail // 8), axis=0)
        for value, (at, n) in zip(values, self.spans):
            code = encode(value, factor)
            if n % 16:
                code = jnp.concatenate([code, rest], axis=0)
            ref[at : at + code.shape[0], :] = code.astype(jnp.bfloat16)
        if self.body % 16 == 0:
            ref[self.body : self.rows, :] = rest.astype(jnp.bfloat16)


def add(some, more):
    return [x + y for x, y in zip(some, more)]


PACKETS = tuple(Packet((112,) * (n // 2) + (56,) * (n % 2)) for _, _, n in STREAMS)
SWAPS = tuple(Packet((32,) * n) for _, _, n in STREAMS)


def kernel(nz, acts_ref, out_ref, mine, pair, other, part0, part1, *rest):
    ns = len(STREAMS)
    got, put, late_got, late_put = (rest[k * ns : (k + 1) * ns] for k in range(4))
    kept, load_sem, psend, precv, wsend, wrecv, rsend, rrecv, lsend, lrecv = rest[4 * ns :]
    parts = (part0, part1)
    chunk = ROWS // nz
    depth = nz // 2

    dp = lax.axis_index("dp")
    t = lax.axis_index("tensor")
    ndp = 2 * nz
    nt = lax.axis_size("tensor")
    z, xh = lax.div(dp, 2), lax.rem(dp, 2)
    core = lax.rem(t, 2)
    even = xh == 0

    def along(hops):
        return (lax.rem(dp + 2 * hops + 2 * ndp, ndp), t)

    twin = dp + 1 - 2 * xh
    across = (twin, t)
    mate = t + 1 - 2 * core
    right, left = lax.rem(t + 2, nt), lax.rem(t + nt - 2, nt)

    load = pltpu.make_async_copy(acts_ref.at[:, 0:COLS], mine, load_sem)
    load.start()
    barrier = pltpu.get_barrier_semaphore()
    partners = [along(sign * jump) for jump in JUMPS for sign in (1, -1)]
    partners += [across, (dp, mate), (twin, mate), (dp, right), (dp, left)]
    for device in partners:
        pl.semaphore_signal(barrier, inc=1, device_id=device, device_id_type=MESH)
    load.wait()
    for i in range(ns):
        for d in range(2):
            got[i][d, depth] = jnp.zeros(got[i].shape[2:], jnp.bfloat16)

    def own_rows(i, owner):
        tile, first, _ = STREAMS[i]
        rows = pl.ds(pl.multiple_of(owner * chunk, 8), chunk)
        values = []
        for at, n in PACKETS[i].spans:
            j = first + at // chunk
            pieces = [
                parts[tile][rows, (j + m) * LANES : (j + m + 1) * LANES] for m in range(n // chunk)
            ]
            values.append(jnp.concatenate(pieces, axis=0) if len(pieces) > 1 else pieces[0])
        return values

    second = [tile for tile, _, _ in STREAMS].index(1)

    def columns(i):
        _, first, blocks = STREAMS[i]
        return first * LANES, (first + blocks) * LANES

    def multiply(i, left_ref, right_ref):
        a, b = columns(i)
        parts[STREAMS[i][0]][:, a:b] = lax.dot_general(
            left_ref[...], right_ref[:, a:b], TN, preferred_element_type=jnp.float32
        )

    pl.semaphore_wait(barrier, len(partners))

    exchange = pltpu.make_async_remote_copy(
        src_ref=mine,
        dst_ref=pair,
        send_sem=psend,
        recv_sem=precv,
        device_id=(dp, mate),
        device_id_type=MESH,
    )
    exchange.start()

    def window(i):
        a, b = columns(i)
        return pltpu.make_async_remote_copy(
            src_ref=mine.at[:, a:b],
            dst_ref=other.at[:, a:b],
            send_sem=wsend.at[i],
            recv_sem=wrecv.at[i],
            device_id=(dp, right),
            device_id_type=MESH,
        )

    @pl.when(core == 1)
    def _():
        for i in range(second, ns):
            window(i).start()

    for i in range(second):
        multiply(i, mine, mine)

    def reach(i, d):
        return depth - lax.rem(d + i, 2)

    def chain(i):
        return by_core(core, [c[i] for c in CHAINS])

    def message(i, d, hop, target):
        return pltpu.make_async_remote_copy(
            src_ref=put[i].at[d, hop - 1],
            dst_ref=got[i].at[d, hop - 1],
            send_sem=rsend.at[i, d, hop - 1],
            recv_sem=rrecv.at[i, d, hop - 1],
            device_id=target,
            device_id_type=MESH,
        )

    def late(i, which):
        target = (twin if which else dp, mate if STREAMS[i][0] else t)
        return pltpu.make_async_remote_copy(
            src_ref=late_put[i].at[which],
            dst_ref=late_got[i].at[which],
            send_sem=lsend.at[i, which],
            recv_sem=lrecv.at[i, which],
            device_id=target,
            device_id_type=MESH,
        )

    def step(i, d, hop, length):
        sign = 1 - 2 * d
        owner = lax.rem(z + sign * hop + nz, nz)
        outermost = (hop == reach(i, d)) | (lax.rem(hop, length) == 0)

        @pl.when(jnp.logical_not(outermost))
        def _():
            message(i, d, hop + 1, across).wait_recv()

        values = own_rows(i, owner)
        bound = tops(values)
        more, more_bound = PACKETS[i].read(got[i].at[d, jnp.where(outermost, depth, hop)])
        PACKETS[i].write(add(values, more), put[i].at[d, hop - 1], bound + more_bound)
        jump = jnp.where(lax.rem(hop, length) == 1, hop, 1)
        message(i, d, hop, along(sign * jump)).start()

    def tick_of(i, k):
        length = chain(i)

        def one(j, _):
            d, m = lax.rem(j, 2), lax.div(j, 2)
            hop = (m + 1) * length - k

            @pl.when((k >= 0) & (k < length) & (hop <= reach(i, d)))
            def _():
                step(i, d, hop, length)

            return 0

        lax.fori_loop(0, 2 * PIECES, one, 0)

    def gather(i):
        length = chain(i)
        values = own_rows(i, z)
        bound = tops(values)
        for m in range(PIECES):
            for d in range(2):
                hop = m * length + 1
                here = hop <= reach(i, d)

                @pl.when(here)
                def _():
                    message(i, d, hop, across).wait_recv()

                more, more_bound = PACKETS[i].read(got[i].at[d, jnp.where(here, hop - 1, depth)])
                values, bound = add(values, more), bound + more_bound
        return values, bound

    inverse = 1.0 / (1024 * ndp)

    def finish(i):
        tile, _, blocks = STREAMS[i]
        values, bound = gather(i)
        total = jnp.concatenate(values, axis=0)
        here, away = [], []
        for block in range(blocks):
            low = total[block * chunk : block * chunk + 32]
            high = total[(block + 1) * chunk - 32 : (block + 1) * chunk]
            here.append(jnp.where(even, low, high))
            away.append(jnp.where(even, high, low))
        SWAPS[i].write(away, late_put[i].at[1], bound)
        late(i, 1).start()
        if tile:
            SWAPS[i].write(here, late_put[i].at[0], bound)
            late(i, 0).start()
        else:
            for block in range(blocks):
                at = 32 * (STREAMS[i][1] + block)
                kept[at : at + 32, :] = here[block]

    def deliver(i):
        tile, first, blocks = STREAMS[i]
        late(i, 1).wait_recv()
        values, _ = SWAPS[i].read(late_got[i].at[1])
        if tile:
            late(i, 0).wait_recv()
            others, _ = SWAPS[i].read(late_got[i].at[0])
        else:
            others = [kept[32 * j : 32 * j + 32, :] for j in range(first, first + blocks)]
        for block in range(blocks):
            total = values[block] + others[block]
            value = jnp.where(even, total[:28], total[4:])
            at = (first + block) * LANES
            out_ref[:, tile, at : at + LANES] = value * inverse

    def tick(now, _):
        for i in range(ns):
            k = now - by_core(core, [s[i] for s in STARTS])
            length = chain(i)

            if STREAMS[i][0]:

                @pl.when(k == 0)
                def _():
                    if i == second:
                        exchange.wait_recv()

                    @pl.when(core == 0)
                    def _():
                        multiply(i, pair, mine)

                    @pl.when(core == 1)
                    def _():
                        window(i).wait_recv()
                        multiply(i, pair, other)


            tick_of(i, k)

            @pl.when(k == length)
            def _():
                finish(i)

            if STREAMS[i][0] == 0:

                @pl.when(k == length + 1)
                def _():
                    deliver(i)

        return 0

    lax.fori_loop(0, TICKS, tick, 0)

    for i in range(second, ns):
        deliver(i)
    exchange.wait_send()

    @pl.when(core == 1)
    def _():
        for i in range(second, ns):
            window(i).wait_send()

    for i in range(ns):
        for d in range(2):

            def sent(k, _):
                message(i, d, k + 1, across).wait_send()
                return 0

            lax.fori_loop(0, depth - (d + i) % 2, sent, 0)
        late(i, 1).wait_send()
        if STREAMS[i][0]:
            late(i, 0).wait_send()


def per_device(acts):
    nz = lax.axis_size("dp") // 2
    depth = nz // 2
    ns = len(STREAMS)
    ring = [p.rows for p in PACKETS]
    swaps = [p.rows for p in SWAPS]
    scratch = [
        pltpu.VMEM((acts.shape[0], COLS), jnp.bfloat16),
        pltpu.VMEM((acts.shape[0], COLS), jnp.bfloat16),
        pltpu.VMEM((acts.shape[0], COLS), jnp.bfloat16),
        pltpu.VMEM((ROWS, COLS), jnp.float32),
        pltpu.VMEM((ROWS, COLS), jnp.float32),
    ]
    scratch += [pltpu.VMEM((2, depth + 1, n, LANES), jnp.bfloat16) for n in ring]
    scratch += [pltpu.VMEM((2, depth, n, LANES), jnp.bfloat16) for n in ring]
    scratch += [pltpu.VMEM((2, n, LANES), jnp.bfloat16) for n in swaps] * 2
    scratch += [pltpu.VMEM((32 * BLOCKS, LANES), jnp.float32)]
    dma = pltpu.SemaphoreType.DMA
    scratch += [dma, dma, dma, dma((ns,)), dma((ns,)), dma((ns, 2, depth)), dma((ns, 2, depth)), dma((ns, 2)), dma((ns, 2))]
    half = ROWS // (2 * nz)
    tiles = pl.pallas_call(
        lambda *refs: kernel(nz, *refs),
        out_shape=jax.ShapeDtypeStruct((half, 2, COLS), jnp.float32),
        in_specs=[pl.BlockSpec(memory_space=pl.ANY)],
        out_specs=pl.BlockSpec(memory_space=pltpu.VMEM),
        scratch_shapes=scratch,
        compiler_params=pltpu.CompilerParams(
            collective_id=0, has_side_effects=True, vmem_limit_bytes=52 * 2**20
        ),
        cost_estimate=pl.CostEstimate(
            flops=4 * ROWS * COLS * acts.shape[0], bytes_accessed=2 * acts.size, transcendentals=0
        ),
    )(acts)
    return tiles.reshape(half, 1, 2, COLS)


def solution(mesh):
    return jax.shard_map(
        per_device,
        mesh=mesh,
        in_specs=(P("dp", "tensor"),),
        out_specs=P("dp", "tensor", None, None),
        check_vma=False,
    )
```

```python
import jax
import jax.numpy as jnp
from jax import lax
from jax.experimental import pallas as pl
from jax.experimental.pallas import tpu as pltpu
from jax.sharding import PartitionSpec as P

ROWS = 896
COLS = 896
LANES = 128
BLOCKS = COLS // LANES
MESH = pl.DeviceIdType.MESH
TN = (((0,), (0,)), ((), ()))

POWER = 17
TOP = 2.0**7.375

STREAMS = ((0, 0, 4), (0, 4, 3), (1, 0, 3), (1, 3, 4))
STARTS = ((0, 0, 0, 0), (0, 0, 2, 5))
CHAINS = ((8, 8, 8, 8), (8, 8, 8, 4))
PIECES = 2
JUMPS = (1, 5)
TICKS = 12


def by_core(core, table):
    return jnp.where(core == 0, table[0], table[1])


def scaled(value, factor):
    return (value.reshape(value.shape[0] // 8, 8, LANES) * factor).reshape(value.shape)


def encode(value, factor):
    u = scaled(value, factor)
    u2 = u * u
    u4 = u2 * u2
    u8 = u4 * u4
    return u8 * u8 * u


def decode(code, factor):
    y = code.astype(jnp.float32)
    size = scaled(jnp.exp2(jnp.log2(jnp.abs(y)) * (1.0 / POWER)), factor)
    return jnp.where(y < 0.0, -size, size)


def tops(values):
    out = None
    for value in values:
        top = jnp.max(jnp.abs(value).reshape(value.shape[0] // 8, 8, LANES), axis=0)
        out = top if out is None else jnp.maximum(out, top)
    return out


class Packet:
    def __init__(self, sizes):
        self.spans = []
        at = 0
        for n in sizes:
            self.spans.append((at, n))
            at += n
        self.body = at
        self.rows = (at // 16 + 1) * 16
        self.tail = self.rows - at

    def read(self, ref):
        bound = ref[self.rows - 16 : self.rows, :].astype(jnp.float32)[8:]
        factor = bound * (1.0 / TOP)
        values = [decode(ref[at : at + (n + 15) // 16 * 16, :], factor)[:n] for at, n in self.spans]
        return values, bound

    def write(self, values, ref, bound):
        bound = (bound * 1.008 + 1e-36).astype(jnp.bfloat16).astype(jnp.float32)
        factor = TOP / bound
        rest = jnp.concatenate([bound] * (self.tail // 8), axis=0)
        for value, (at, n) in zip(values, self.spans):
            code = encode(value, factor)
            if n % 16:
                code = jnp.concatenate([code, rest], axis=0)
            ref[at : at + code.shape[0], :] = code.astype(jnp.bfloat16)
        if self.body % 16 == 0:
            ref[self.body : self.rows, :] = rest.astype(jnp.bfloat16)


def add(some, more):
    return [x + y for x, y in zip(some, more)]


PACKETS = tuple(Packet((112,) * (n // 2) + (56,) * (n % 2)) for _, _, n in STREAMS)
SWAPS = tuple(Packet((32,) * n) for _, _, n in STREAMS)


def kernel(nz, acts_ref, out_ref, mine, pair, other, part0, part1, *rest):
    ns = len(STREAMS)
    got, put, late_got, late_put = (rest[k * ns : (k + 1) * ns] for k in range(4))
    kept, load_sem, psend, precv, wsend, wrecv, rsend, rrecv, lsend, lrecv = rest[4 * ns :]
    parts = (part0, part1)
    chunk = ROWS // nz
    depth = nz // 2

    dp = lax.axis_index("dp")
    t = lax.axis_index("tensor")
    ndp = 2 * nz
    nt = lax.axis_size("tensor")
    z, xh = lax.div(dp, 2), lax.rem(dp, 2)
    core = lax.rem(t, 2)
    even = xh == 0

    def along(hops):
        return (lax.rem(dp + 2 * hops + 2 * ndp, ndp), t)

    twin = dp + 1 - 2 * xh
    across = (twin, t)
    mate = t + 1 - 2 * core
    right, left = lax.rem(t + 2, nt), lax.rem(t + nt - 2, nt)

    load = pltpu.make_async_copy(acts_ref.at[:, 0:COLS], mine, load_sem)
    load.start()
    barrier = pltpu.get_barrier_semaphore()
    partners = [along(sign * jump) for jump in JUMPS for sign in (1, -1)]
    partners += [across, (dp, mate), (twin, mate), (dp, right), (dp, left)]
    for device in partners:
        pl.semaphore_signal(barrier, inc=1, device_id=device, device_id_type=MESH)
    load.wait()
    for i in range(ns):
        for d in range(2):
            got[i][d, depth] = jnp.zeros(got[i].shape[2:], jnp.bfloat16)

    def own_rows(i, owner):
        tile, first, _ = STREAMS[i]
        rows = pl.ds(pl.multiple_of(owner * chunk, 8), chunk)
        values = []
        for at, n in PACKETS[i].spans:
            j = first + at // chunk
            pieces = [
                parts[tile][rows, (j + m) * LANES : (j + m + 1) * LANES] for m in range(n // chunk)
            ]
            values.append(jnp.concatenate(pieces, axis=0) if len(pieces) > 1 else pieces[0])
        return values

    second = [tile for tile, _, _ in STREAMS].index(1)

    def columns(i):
        _, first, blocks = STREAMS[i]
        return first * LANES, (first + blocks) * LANES

    def multiply(i, left_ref, right_ref):
        a, b = columns(i)
        parts[STREAMS[i][0]][:, a:b] = lax.dot_general(
            left_ref[...], right_ref[:, a:b], TN, preferred_element_type=jnp.float32
        )

    pl.semaphore_wait(barrier, len(partners))

    exchange = pltpu.make_async_remote_copy(
        src_ref=mine,
        dst_ref=pair,
        send_sem=psend,
        recv_sem=precv,
        device_id=(dp, mate),
        device_id_type=MESH,
    )
    exchange.start()

    def window(i):
        a, b = columns(i)
        return pltpu.make_async_remote_copy(
            src_ref=mine.at[:, a:b],
            dst_ref=other.at[:, a:b],
            send_sem=wsend.at[i],
            recv_sem=wrecv.at[i],
            device_id=(dp, right),
            device_id_type=MESH,
        )

    @pl.when(core == 1)
    def _():
        for i in range(second, ns):
            window(i).start()

    part0[...] = lax.dot_general(mine[...], mine[...], TN, preferred_element_type=jnp.float32)

    def reach(i, d):
        return depth - lax.rem(d + i, 2)

    def chain(i):
        return by_core(core, [c[i] for c in CHAINS])

    def message(i, d, hop, target):
        return pltpu.make_async_remote_copy(
            src_ref=put[i].at[d, hop - 1],
            dst_ref=got[i].at[d, hop - 1],
            send_sem=rsend.at[i, d, hop - 1],
            recv_sem=rrecv.at[i, d, hop - 1],
            device_id=target,
            device_id_type=MESH,
        )

    def late(i, which):
        target = (twin if which else dp, mate if STREAMS[i][0] else t)
        return pltpu.make_async_remote_copy(
            src_ref=late_put[i].at[which],
            dst_ref=late_got[i].at[which],
            send_sem=lsend.at[i, which],
            recv_sem=lrecv.at[i, which],
            device_id=target,
            device_id_type=MESH,
        )

    def step(i, d, hop, length):
        sign = 1 - 2 * d
        owner = lax.rem(z + sign * hop + nz, nz)
        outermost = (hop == reach(i, d)) | (lax.rem(hop, length) == 0)

        @pl.when(jnp.logical_not(outermost))
        def _():
            message(i, d, hop + 1, across).wait_recv()

        values = own_rows(i, owner)
        bound = tops(values)
        more, more_bound = PACKETS[i].read(got[i].at[d, jnp.where(outermost, depth, hop)])
        PACKETS[i].write(add(values, more), put[i].at[d, hop - 1], bound + more_bound)
        jump = jnp.where(lax.rem(hop, length) == 1, hop, 1)
        message(i, d, hop, along(sign * jump)).start()

    def tick_of(i, k):
        length = chain(i)

        def one(j, _):
            d, m = lax.rem(j, 2), lax.div(j, 2)
            hop = (m + 1) * length - k

            @pl.when((k >= 0) & (k < length) & (hop <= reach(i, d)))
            def _():
                step(i, d, hop, length)

            return 0

        lax.fori_loop(0, 2 * PIECES, one, 0)

    def gather(i):
        length = chain(i)
        values = own_rows(i, z)
        bound = tops(values)
        for m in range(PIECES):
            for d in range(2):
                hop = m * length + 1
                here = hop <= reach(i, d)

                @pl.when(here)
                def _():
                    message(i, d, hop, across).wait_recv()

                more, more_bound = PACKETS[i].read(got[i].at[d, jnp.where(here, hop - 1, depth)])
                values, bound = add(values, more), bound + more_bound
        return values, bound

    inverse = 1.0 / (1024 * ndp)

    def finish(i):
        tile, _, blocks = STREAMS[i]
        values, bound = gather(i)
        total = jnp.concatenate(values, axis=0)
        here, away = [], []
        for block in range(blocks):
            low = total[block * chunk : block * chunk + 32]
            high = total[(block + 1) * chunk - 32 : (block + 1) * chunk]
            here.append(jnp.where(even, low, high))
            away.append(jnp.where(even, high, low))
        SWAPS[i].write(away, late_put[i].at[1], bound)
        late(i, 1).start()
        if tile:
            SWAPS[i].write(here, late_put[i].at[0], bound)
            late(i, 0).start()
        else:
            for block in range(blocks):
                at = 32 * (STREAMS[i][1] + block)
                kept[at : at + 32, :] = here[block]

    def deliver(i):
        tile, first, blocks = STREAMS[i]
        late(i, 1).wait_recv()
        values, _ = SWAPS[i].read(late_got[i].at[1])
        if tile:
            late(i, 0).wait_recv()
            others, _ = SWAPS[i].read(late_got[i].at[0])
        else:
            others = [kept[32 * j : 32 * j + 32, :] for j in range(first, first + blocks)]
        for block in range(blocks):
            total = values[block] + others[block]
            value = jnp.where(even, total[:28], total[4:])
            at = (first + block) * LANES
            out_ref[:, tile, at : at + LANES] = value * inverse

    def tick(now, _):
        for i in range(ns):
            k = now - by_core(core, [s[i] for s in STARTS])
            length = chain(i)

            if STREAMS[i][0]:

                @pl.when(k == 0)
                def _():
                    if i == second:
                        exchange.wait_recv()

                    @pl.when(core == 0)
                    def _():
                        multiply(i, pair, mine)

                    @pl.when(core == 1)
                    def _():
                        window(i).wait_recv()
                        multiply(i, pair, other)


            tick_of(i, k)

            @pl.when(k == length)
            def _():
                finish(i)

            if STREAMS[i][0] == 0:

                @pl.when(k == length + 1)
                def _():
                    deliver(i)

        return 0

    lax.fori_loop(0, TICKS, tick, 0)

    for i in range(second, ns):
        deliver(i)
    exchange.wait_send()

    @pl.when(core == 1)
    def _():
        for i in range(second, ns):
            window(i).wait_send()

    for i in range(ns):
        for d in range(2):

            def sent(k, _):
                message(i, d, k + 1, across).wait_send()
                return 0

            lax.fori_loop(0, depth - (d + i) % 2, sent, 0)
        late(i, 1).wait_send()
        if STREAMS[i][0]:
            late(i, 0).wait_send()


def per_device(acts):
    nz = lax.axis_size("dp") // 2
    depth = nz // 2
    ns = len(STREAMS)
    ring = [p.rows for p in PACKETS]
    swaps = [p.rows for p in SWAPS]
    scratch = [
        pltpu.VMEM((acts.shape[0], COLS), jnp.bfloat16),
        pltpu.VMEM((acts.shape[0], COLS), jnp.bfloat16),
        pltpu.VMEM((acts.shape[0], COLS), jnp.bfloat16),
        pltpu.VMEM((ROWS, COLS), jnp.float32),
        pltpu.VMEM((ROWS, COLS), jnp.float32),
    ]
    scratch += [pltpu.VMEM((2, depth + 1, n, LANES), jnp.bfloat16) for n in ring]
    scratch += [pltpu.VMEM((2, depth, n, LANES), jnp.bfloat16) for n in ring]
    scratch += [pltpu.VMEM((2, n, LANES), jnp.bfloat16) for n in swaps] * 2
    scratch += [pltpu.VMEM((32 * BLOCKS, LANES), jnp.float32)]
    dma = pltpu.SemaphoreType.DMA
    scratch += [dma, dma, dma, dma((ns,)), dma((ns,)), dma((ns, 2, depth)), dma((ns, 2, depth)), dma((ns, 2)), dma((ns, 2))]
    half = ROWS // (2 * nz)
    tiles = pl.pallas_call(
        lambda *refs: kernel(nz, *refs),
        out_shape=jax.ShapeDtypeStruct((half, 2, COLS), jnp.float32),
        in_specs=[pl.BlockSpec(memory_space=pl.ANY)],
        out_specs=pl.BlockSpec(memory_space=pltpu.VMEM),
        scratch_shapes=scratch,
        compiler_params=pltpu.CompilerParams(
            collective_id=0, has_side_effects=True, vmem_limit_bytes=52 * 2**20
        ),
        cost_estimate=pl.CostEstimate(
            flops=4 * ROWS * COLS * acts.shape[0], bytes_accessed=2 * acts.size, transcendentals=0
        ),
    )(acts)
    return tiles.reshape(half, 1, 2, COLS)


def solution(mesh):
    return jax.shard_map(
        per_device,
        mesh=mesh,
        in_specs=(P("dp", "tensor"),),
        out_specs=P("dp", "tensor", None, None),
        check_vma=False,
    )
```

```python
import jax
import jax.numpy as jnp
from jax import lax
from jax.experimental import pallas as pl
from jax.experimental.pallas import tpu as pltpu
from jax.sharding import PartitionSpec as P

ROWS = 896
COLS = 896
LANES = 128
BLOCKS = COLS // LANES
MESH = pl.DeviceIdType.MESH
TN = (((0,), (0,)), ((), ()))

POWER = 17
TOP = 2.0**7.375

STREAMS = ((0, 0, 4), (0, 4, 3), (1, 0, 3), (1, 3, 4))
STARTS = ((0, 0, 0, 1), (0, 0, 2, 5))
CHAINS = ((8, 8, 8, 8), (8, 8, 8, 4))
PIECES = 2
JUMPS = (1, 5)
TICKS = 12


def by_core(core, table):
    return jnp.where(core == 0, table[0], table[1])


def scaled(value, factor):
    return (value.reshape(value.shape[0] // 8, 8, LANES) * factor).reshape(value.shape)


def encode(value, factor):
    u = scaled(value, factor)
    u2 = u * u
    u4 = u2 * u2
    u8 = u4 * u4
    return u8 * u8 * u


def decode(code, factor):
    y = code.astype(jnp.float32)
    size = scaled(jnp.exp2(jnp.log2(jnp.abs(y)) * (1.0 / POWER)), factor)
    return jnp.where(y < 0.0, -size, size)


def tops(values):
    out = None
    for value in values:
        top = jnp.max(jnp.abs(value).reshape(value.shape[0] // 8, 8, LANES), axis=0)
        out = top if out is None else jnp.maximum(out, top)
    return out


class Packet:
    def __init__(self, sizes):
        self.spans = []
        at = 0
        for n in sizes:
            self.spans.append((at, n))
            at += n
        self.body = at
        self.rows = (at // 16 + 1) * 16
        self.tail = self.rows - at

    def read(self, ref):
        bound = ref[self.rows - 16 : self.rows, :].astype(jnp.float32)[8:]
        factor = bound * (1.0 / TOP)
        values = [decode(ref[at : at + (n + 15) // 16 * 16, :], factor)[:n] for at, n in self.spans]
        return values, bound

    def write(self, values, ref, bound):
        bound = (bound * 1.008 + 1e-36).astype(jnp.bfloat16).astype(jnp.float32)
        factor = TOP / bound
        rest = jnp.concatenate([bound] * (self.tail // 8), axis=0)
        for value, (at, n) in zip(values, self.spans):
            code = encode(value, factor)
            if n % 16:
                code = jnp.concatenate([code, rest], axis=0)
            ref[at : at + code.shape[0], :] = code.astype(jnp.bfloat16)
        if self.body % 16 == 0:
            ref[self.body : self.rows, :] = rest.astype(jnp.bfloat16)


def add(some, more):
    return [x + y for x, y in zip(some, more)]


PACKETS = tuple(Packet((112,) * (n // 2) + (56,) * (n % 2)) for _, _, n in STREAMS)
SWAPS = tuple(Packet((32,) * n) for _, _, n in STREAMS)


def kernel(nz, acts_ref, out_ref, mine, pair, other, part0, part1, *rest):
    ns = len(STREAMS)
    got, put, late_got, late_put = (rest[k * ns : (k + 1) * ns] for k in range(4))
    kept, load_sem, psend, precv, wsend, wrecv, rsend, rrecv, lsend, lrecv = rest[4 * ns :]
    parts = (part0, part1)
    chunk = ROWS // nz
    depth = nz // 2

    dp = lax.axis_index("dp")
    t = lax.axis_index("tensor")
    ndp = 2 * nz
    nt = lax.axis_size("tensor")
    z, xh = lax.div(dp, 2), lax.rem(dp, 2)
    core = lax.rem(t, 2)
    even = xh == 0

    def along(hops):
        return (lax.rem(dp + 2 * hops + 2 * ndp, ndp), t)

    twin = dp + 1 - 2 * xh
    across = (twin, t)
    mate = t + 1 - 2 * core
    right, left = lax.rem(t + 2, nt), lax.rem(t + nt - 2, nt)

    load = pltpu.make_async_copy(acts_ref.at[:, 0:COLS], mine, load_sem)
    load.start()
    barrier = pltpu.get_barrier_semaphore()
    partners = [along(sign * jump) for jump in JUMPS for sign in (1, -1)]
    partners += [across, (dp, mate), (twin, mate), (dp, right), (dp, left)]
    for device in partners:
        pl.semaphore_signal(barrier, inc=1, device_id=device, device_id_type=MESH)
    load.wait()
    for i in range(ns):
        for d in range(2):
            got[i][d, depth] = jnp.zeros(got[i].shape[2:], jnp.bfloat16)

    def own_rows(i, owner):
        tile, first, _ = STREAMS[i]
        rows = pl.ds(pl.multiple_of(owner * chunk, 8), chunk)
        values = []
        for at, n in PACKETS[i].spans:
            j = first + at // chunk
            pieces = [
                parts[tile][rows, (j + m) * LANES : (j + m + 1) * LANES] for m in range(n // chunk)
            ]
            values.append(jnp.concatenate(pieces, axis=0) if len(pieces) > 1 else pieces[0])
        return values

    second = [tile for tile, _, _ in STREAMS].index(1)

    def columns(i):
        _, first, blocks = STREAMS[i]
        return first * LANES, (first + blocks) * LANES

    def multiply(i, left_ref, right_ref):
        a, b = columns(i)
        parts[STREAMS[i][0]][:, a:b] = lax.dot_general(
            left_ref[...], right_ref[:, a:b], TN, preferred_element_type=jnp.float32
        )

    pl.semaphore_wait(barrier, len(partners))

    exchange = pltpu.make_async_remote_copy(
        src_ref=mine,
        dst_ref=pair,
        send_sem=psend,
        recv_sem=precv,
        device_id=(dp, mate),
        device_id_type=MESH,
    )
    exchange.start()

    def window(i):
        a, b = columns(i)
        return pltpu.make_async_remote_copy(
            src_ref=mine.at[:, a:b],
            dst_ref=other.at[:, a:b],
            send_sem=wsend.at[i],
            recv_sem=wrecv.at[i],
            device_id=(dp, right),
            device_id_type=MESH,
        )

    @pl.when(core == 1)
    def _():
        for i in range(second, ns):
            window(i).start()

    for i in range(second):
        multiply(i, mine, mine)

    def reach(i, d):
        return depth - lax.rem(d + i, 2)

    def chain(i):
        return by_core(core, [c[i] for c in CHAINS])

    def message(i, d, hop, target):
        return pltpu.make_async_remote_copy(
            src_ref=put[i].at[d, hop - 1],
            dst_ref=got[i].at[d, hop - 1],
            send_sem=rsend.at[i, d, hop - 1],
            recv_sem=rrecv.at[i, d, hop - 1],
            device_id=target,
            device_id_type=MESH,
        )

    def late(i, which):
        target = (twin if which else dp, mate if STREAMS[i][0] else t)
        return pltpu.make_async_remote_copy(
            src_ref=late_put[i].at[which],
            dst_ref=late_got[i].at[which],
            send_sem=lsend.at[i, which],
            recv_sem=lrecv.at[i, which],
            device_id=target,
            device_id_type=MESH,
        )

    def step(i, d, hop, length):
        sign = 1 - 2 * d
        owner = lax.rem(z + sign * hop + nz, nz)
        outermost = (hop == reach(i, d)) | (lax.rem(hop, length) == 0)

        @pl.when(jnp.logical_not(outermost))
        def _():
            message(i, d, hop + 1, across).wait_recv()

        values = own_rows(i, owner)
        bound = tops(values)
        more, more_bound = PACKETS[i].read(got[i].at[d, jnp.where(outermost, depth, hop)])
        PACKETS[i].write(add(values, more), put[i].at[d, hop - 1], bound + more_bound)
        jump = jnp.where(lax.rem(hop, length) == 1, hop, 1)
        message(i, d, hop, along(sign * jump)).start()

    def tick_of(i, k):
        length = chain(i)

        def one(j, _):
            d, m = lax.rem(j, 2), lax.div(j, 2)
            hop = (m + 1) * length - k

            @pl.when((k >= 0) & (k < length) & (hop <= reach(i, d)))
            def _():
                step(i, d, hop, length)

            return 0

        lax.fori_loop(0, 2 * PIECES, one, 0)

    def gather(i):
        length = chain(i)
        values = own_rows(i, z)
        bound = tops(values)
        for m in range(PIECES):
            for d in range(2):
                hop = m * length + 1
                here = hop <= reach(i, d)

                @pl.when(here)
                def _():
                    message(i, d, hop, across).wait_recv()

                more, more_bound = PACKETS[i].read(got[i].at[d, jnp.where(here, hop - 1, depth)])
                values, bound = add(values, more), bound + more_bound
        return values, bound

    inverse = 1.0 / (1024 * ndp)

    def finish(i):
        tile, _, blocks = STREAMS[i]
        values, bound = gather(i)
        total = jnp.concatenate(values, axis=0)
        here, away = [], []
        for block in range(blocks):
            low = total[block * chunk : block * chunk + 32]
            high = total[(block + 1) * chunk - 32 : (block + 1) * chunk]
            here.append(jnp.where(even, low, high))
            away.append(jnp.where(even, high, low))
        SWAPS[i].write(away, late_put[i].at[1], bound)
        late(i, 1).start()
        if tile:
            SWAPS[i].write(here, late_put[i].at[0], bound)
            late(i, 0).start()
        else:
            for block in range(blocks):
                at = 32 * (STREAMS[i][1] + block)
                kept[at : at + 32, :] = here[block]

    def deliver(i):
        tile, first, blocks = STREAMS[i]
        late(i, 1).wait_recv()
        values, _ = SWAPS[i].read(late_got[i].at[1])
        if tile:
            late(i, 0).wait_recv()
            others, _ = SWAPS[i].read(late_got[i].at[0])
        else:
            others = [kept[32 * j : 32 * j + 32, :] for j in range(first, first + blocks)]
        for block in range(blocks):
            total = values[block] + others[block]
            value = jnp.where(even, total[:28], total[4:])
            at = (first + block) * LANES
            out_ref[:, tile, at : at + LANES] = value * inverse

    def tick(now, _):
        for i in range(ns):
            k = now - by_core(core, [s[i] for s in STARTS])
            length = chain(i)

            if STREAMS[i][0]:

                @pl.when(k == 0)
                def _():
                    if i == second:
                        exchange.wait_recv()

                    @pl.when(core == 0)
                    def _():
                        multiply(i, pair, mine)

                    @pl.when(core == 1)
                    def _():
                        window(i).wait_recv()
                        multiply(i, pair, other)


            tick_of(i, k)

            @pl.when(k == length)
            def _():
                finish(i)

            if STREAMS[i][0] == 0:

                @pl.when(k == length + 1)
                def _():
                    deliver(i)

        return 0

    lax.fori_loop(0, TICKS, tick, 0)

    for i in range(second, ns):
        deliver(i)
    exchange.wait_send()

    @pl.when(core == 1)
    def _():
        for i in range(second, ns):
            window(i).wait_send()

    for i in range(ns):
        for d in range(2):

            def sent(k, _):
                message(i, d, k + 1, across).wait_send()
                return 0

            lax.fori_loop(0, depth - (d + i) % 2, sent, 0)
        late(i, 1).wait_send()
        if STREAMS[i][0]:
            late(i, 0).wait_send()


def per_device(acts):
    nz = lax.axis_size("dp") // 2
    depth = nz // 2
    ns = len(STREAMS)
    ring = [p.rows for p in PACKETS]
    swaps = [p.rows for p in SWAPS]
    scratch = [
        pltpu.VMEM((acts.shape[0], COLS), jnp.bfloat16),
        pltpu.VMEM((acts.shape[0], COLS), jnp.bfloat16),
        pltpu.VMEM((acts.shape[0], COLS), jnp.bfloat16),
        pltpu.VMEM((ROWS, COLS), jnp.float32),
        pltpu.VMEM((ROWS, COLS), jnp.float32),
    ]
    scratch += [pltpu.VMEM((2, depth + 1, n, LANES), jnp.bfloat16) for n in ring]
    scratch += [pltpu.VMEM((2, depth, n, LANES), jnp.bfloat16) for n in ring]
    scratch += [pltpu.VMEM((2, n, LANES), jnp.bfloat16) for n in swaps] * 2
    scratch += [pltpu.VMEM((32 * BLOCKS, LANES), jnp.float32)]
    dma = pltpu.SemaphoreType.DMA
    scratch += [dma, dma, dma, dma((ns,)), dma((ns,)), dma((ns, 2, depth)), dma((ns, 2, depth)), dma((ns, 2)), dma((ns, 2))]
    half = ROWS // (2 * nz)
    tiles = pl.pallas_call(
        lambda *refs: kernel(nz, *refs),
        out_shape=jax.ShapeDtypeStruct((half, 2, COLS), jnp.float32),
        in_specs=[pl.BlockSpec(memory_space=pl.ANY)],
        out_specs=pl.BlockSpec(memory_space=pltpu.VMEM),
        scratch_shapes=scratch,
        compiler_params=pltpu.CompilerParams(
            collective_id=0, has_side_effects=True, vmem_limit_bytes=52 * 2**20
        ),
        cost_estimate=pl.CostEstimate(
            flops=4 * ROWS * COLS * acts.shape[0], bytes_accessed=2 * acts.size, transcendentals=0
        ),
    )(acts)
    return tiles.reshape(half, 1, 2, COLS)


def solution(mesh):
    return jax.shard_map(
        per_device,
        mesh=mesh,
        in_specs=(P("dp", "tensor"),),
        out_specs=P("dp", "tensor", None, None),
        check_vma=False,
    )
```
